32 devices in a mesh: groups: 1, tok: 32 (over z, y, x, core).
Axes of the slice: x: 2, y: 2, z: 4, core: 2. Of those that a mesh axis runs over, the one named last changes fastest.
Arguments:
- acts: bfloat16 [8192, 8192], P(('groups', 'tok')), may hold values from -6 to 6
- grads_out: bfloat16 [8192, 8192], P(('groups', 'tok')), may hold values from -6 to 6
- proj_in: bfloat16 [8192, 64], replicated, may hold values from -0.0625 to 0.0625
- proj_out: bfloat16 [8192, 64], replicated, may hold values from -0.0625 to 0.0625
- lengths: int32 [32], P('groups'), may hold values from 64 to 1024, as said below
- owned: int32 [32], P(('groups', 'tok')), may hold values from 0 to 31, each once
- queries: bfloat16 [128, 4096], P(('groups', 'tok')), may hold values from -6 to 6
Outputs:
- scores: float32 [32, 128], P(('groups', 'tok'))
The draws below stay inside these ranges and needn't reach their ends.
Inputs may be any that keep to these rules, and one draw needn't show every extreme that they name: Sequence 0 has 1024 tokens, sequence 1 has 255, sequences 2 to 5 have 64 each, and all lengths sum to 8192; so no shard of 256 tokens touches more than 5 sequences, and the sixth shard touches exactly 5. `owned`: every sequence index appears exactly once.
All inputs are finite; a program needn't handle non-finite values.
Results may differ from the reference program's by a relative error of at most 0.0029.
Values may be sent and summed in bfloat16 or wider, within the bound.
A program may use at most 64 MiB of HBM per device.

```python
import jax
import jax.numpy as jnp
from jax import lax

D = 8192
R = 64
TOK_DEV = 256
LMIN = 64
LMAX = 1024
PIECES = 5
SEQS = 32
TOKENS = 8192
NQ = 128
N_TOK = 32


def draw_lengths(key, part):
    key = jax.random.fold_in(key, 11)
    head_short = TOK_DEV // LMIN
    rest_count = SEQS - 2 - head_short
    extra_total = TOKENS - LMAX - (TOK_DEV - 1) - head_short * LMIN - rest_count * LMIN
    ceiling_extra = extra_total // rest_count
    base_extra = jax.random.randint(key, (rest_count,), 0, ceiling_extra + 1, dtype=jnp.int32)
    leftover = extra_total - jnp.sum(base_extra)
    bumped = (jnp.arange(rest_count, dtype=jnp.int32) < leftover % rest_count).astype(jnp.int32)
    rest_lengths = (LMIN + base_extra + leftover // rest_count + bumped).astype(jnp.int32)
    head_lengths = jnp.array([LMAX, TOK_DEV - 1], dtype=jnp.int32)
    short_lengths = jnp.full((head_short,), LMIN, jnp.int32)
    return jnp.concatenate([head_lengths, short_lengths, rest_lengths]).astype(jnp.int32)


def shard_levels(own_key, shape, shards, least, largest):
    factor_of = 1.0
    for dim, blocks in shards:
        heights = jax.random.uniform(jax.random.fold_in(jax.random.fold_in(own_key, 6), dim), (blocks,), jnp.float32, least / len(shards), largest / len(shards))
        factor_of = factor_of * jnp.repeat(jnp.exp(heights), shape[dim] // blocks).reshape((-1,) + (1,) * (len(shape) - 1 - dim))
    return factor_of


def noise(own_key, extent, deviation, limit, shards=(), held_as=jnp.bfloat16):
    factor_of = shard_levels(own_key, extent, shards, -0.22, 0.18) if shards else 1.0
    drawn = jax.random.normal(own_key, extent, jnp.float32) * deviation * factor_of
    return jnp.minimum(jnp.maximum(drawn, -limit), limit).astype(held_as)


def setup_inputs(seed: int = 0, part: int = 0) -> dict:
    splits = jax.random.split(jax.random.key(seed), 8)
    part_splits = jax.random.split(jax.random.fold_in(splits[7], part), 8)
    return {
        "acts": noise(part_splits[0], (TOKENS, D), 1.0, 6.0, ((0, 32),)),
        "grads_out": noise(part_splits[1], (TOKENS, D), 1.0, 6.0, ((0, 32),)),
        "proj_in": noise(splits[2], (D, R), D ** -0.5, 0.0625),
        "proj_out": noise(splits[3], (D, R), D ** -0.5, 0.0625),
        "lengths": draw_lengths(jax.random.fold_in(jax.random.fold_in(splits[7], part), 71), part),
        "owned": jax.random.permutation(part_splits[5], SEQS).astype(jnp.int32),
        "queries": noise(part_splits[6], (NQ, R * R), 1.0, 6.0, ((0, 32),)),
    }


def reference(acts, grads_out, proj_in, proj_out, lengths, owned, queries):
    proj_rank = proj_in.shape[1]
    seq_ends = jnp.cumsum(lengths).astype(jnp.int32)
    acts_blocks = acts.reshape(N_TOK, TOK_DEV, D)
    grads_blocks = grads_out.reshape(N_TOK, TOK_DEV, D)
    seq_index = jnp.arange(SEQS, dtype=jnp.int32)

    def shard_step(running, inputs):
        act_blk, grad_blk, shard = inputs
        positions = shard * TOK_DEV + jnp.arange(TOK_DEV, dtype=jnp.int32)
        seq_of = lax.optimization_barrier(jnp.sum((seq_ends[None, :] <= positions[:, None]).astype(jnp.int32), axis=1)).astype(jnp.int32)
        piece_ids = seq_of[0] + jnp.arange(PIECES, dtype=jnp.int32)
        member = (seq_of[:, None] == piece_ids[None, :]).astype(jnp.float32)
        act_proj = jnp.dot(act_blk, proj_in, preferred_element_type=jnp.float32)
        grad_proj = jnp.dot(grad_blk, proj_out, preferred_element_type=jnp.float32)
        outer_terms = (grad_proj[:, :, None] * act_proj[:, None, :]).reshape(TOK_DEV, proj_rank * proj_rank)
        pieces = jnp.dot(member.T, outer_terms, precision=lax.Precision.HIGHEST).astype(jnp.bfloat16)
        hits_mask = (seq_index[:, None] == piece_ids[None, :]).astype(jnp.float32)
        running = running + jnp.dot(hits_mask, pieces.astype(jnp.float32), precision=lax.Precision.HIGHEST)
        return (running, None)
    seq_grads, _ = lax.scan(shard_step, jnp.zeros((SEQS, proj_rank * proj_rank), jnp.float32), (acts_blocks, grads_blocks, jnp.arange(N_TOK, dtype=jnp.int32)))
    scale = 1.0 / (proj_rank * jnp.sqrt(lengths.astype(jnp.float32)))
    chosen = seq_grads[owned] * scale[owned][:, None]
    return jnp.dot(chosen, queries.astype(jnp.float32).T, precision=lax.Precision.HIGHEST)
```

```python
import functools

import jax
import jax.numpy as jnp
from jax import lax
from jax.experimental import pallas as pl
from jax.experimental.pallas import tpu as pltpu
from jax.sharding import PartitionSpec as P

GROUP = 8
ROWS = 8
CHUNKS = 8
NT = (((1,), (1,)), ((), ()))


def split_bf16(x, parts):
    out = []
    for _ in range(parts):
        head = x.astype(jnp.bfloat16)
        out.append(head)
        x = x - head.astype(jnp.float32)
    return out


def kernel(
    n, acts, grads, pin, pout, lengths, owned, queries, out,
    a_buf, g_buf, pi_buf, po_buf, q_f32, q_send, q_recv, q_mat_f32, q_mat,
    o_send, o_recv, o_mat, p_send, p_recv, s_send, s_recv,
    load_sem, q_ssem, q_rsem, o_ssem, o_rsem, p_ssem, p_rsem, s_ssem, s_rsem,
):
    me = lax.axis_index("tok")
    tok, width = a_buf.shape
    rank = pi_buf.shape[0]
    step = width // CHUNKS
    nq_dev = queries.shape[0]
    nq = nq_dev * n
    seqs = lengths.shape[1]
    flat = rank * rank
    span = flat // GROUP
    blocks = span // 128
    base = lax.div(me, GROUP) * GROUP
    slot = lax.rem(me, GROUP)

    loads = []
    for i in range(CHUNKS):
        cols = pl.ds(i * step, step)
        group = [
            pltpu.make_async_copy(src.at[:, cols], dst.at[:, cols], load_sem.at[i, j])
            for j, (src, dst) in enumerate(
                ((pout, po_buf), (grads, g_buf), (pin, pi_buf), (acts, a_buf))
            )
        ]
        for c in group:
            c.start()
        loads.append(group)

    barrier = pltpu.get_barrier_semaphore()

    def greet(i, _):
        pl.semaphore_signal(
            barrier, inc=1, device_id={"tok": lax.rem(me + i, n)},
            device_id_type=pl.DeviceIdType.MESH,
        )
        return 0

    lax.fori_loop(1, n, greet, 0)

    for a in range(GROUP):
        for b in range(blocks):
            q_f32[a, b * nq_dev:(b + 1) * nq_dev, :] = queries[
                :, (a * blocks + b) * 128:(a * blocks + b + 1) * 128
            ].astype(jnp.float32)
    q_send[...] = q_f32[...].astype(jnp.bfloat16)
    own = owned[0]
    o_send[...] = jnp.full(o_send.shape, own, jnp.int32)

    pl.semaphore_wait(barrier, n - 1)

    def send_queries(i, _):
        to = lax.rem(me + i, n)
        pltpu.make_async_remote_copy(
            q_send.at[lax.rem(to, GROUP)], q_recv.at[me], q_ssem, q_rsem,
            device_id={"tok": to}, device_id_type=pl.DeviceIdType.MESH,
        ).start()
        pltpu.make_async_remote_copy(
            o_send.at[0], o_recv.at[me], o_ssem, o_rsem,
            device_id={"tok": to}, device_id_type=pl.DeviceIdType.MESH,
        ).start()
        return 0

    lax.fori_loop(1, n, send_queries, 0)

    len_row = lengths[...].astype(jnp.float32)
    row_i = lax.broadcasted_iota(jnp.int32, (seqs, seqs), 0)
    col_i = lax.broadcasted_iota(jnp.int32, (seqs, seqs), 1)
    ends = jnp.sum(jnp.where(col_i <= row_i, len_row, 0.0), axis=1, keepdims=True)
    pos = (me * tok + lax.broadcasted_iota(jnp.int32, (1, tok), 1)).astype(jnp.float32)
    seq_of = jnp.sum((ends <= pos).astype(jnp.float32), axis=0, keepdims=True)
    start = (me * tok).astype(jnp.float32)
    first = jnp.sum((ends <= start).astype(jnp.float32), axis=0, keepdims=True)
    piece = lax.broadcasted_iota(jnp.int32, (ROWS, tok), 0).astype(jnp.float32)
    member = ((seq_of - first) == piece).astype(jnp.float32)
    lane = lax.broadcasted_iota(jnp.int32, (1, GROUP * ROWS), 1)
    shard_start = ((base + lane // ROWS) * tok).astype(jnp.float32)
    ids = jnp.sum((ends <= shard_start).astype(jnp.float32), axis=0, keepdims=True)
    ids = ids + (lane % ROWS).astype(jnp.float32)

    g_t = jnp.zeros((rank, tok), jnp.float32)
    a_t = jnp.zeros((rank, tok), jnp.float32)
    for i in range(CHUNKS):
        cols = pl.ds(i * step, step)
        loads[i][0].wait()
        loads[i][1].wait()
        g_t += lax.dot_general(
            po_buf[:, cols], g_buf[:, cols], NT, preferred_element_type=jnp.float32
        )
        loads[i][2].wait()
        loads[i][3].wait()
        a_t += lax.dot_general(
            pi_buf[:, cols], a_buf[:, cols], NT, preferred_element_type=jnp.float32
        )

    g_hi, g_lo = [
        (part.astype(jnp.float32)[:, None, :] * member[None]).reshape(rank * ROWS, tok)
        .astype(jnp.bfloat16)
        for part in split_bf16(g_t, 2)
    ]
    a_hi, a_lo = split_bf16(a_t, 2)
    both = jnp.concatenate([a_hi, a_hi, a_lo, a_lo], axis=0)
    m = lax.dot_general(g_hi, both, NT, preferred_element_type=jnp.float32)
    m = m[:, :2 * rank] + m[:, 2 * rank:] + lax.dot_general(
        g_lo, both[:2 * rank], NT, preferred_element_type=jnp.float32
    )
    m = m.reshape(rank // 2, 2, ROWS, 2 * rank)
    low = lax.broadcasted_iota(jnp.int32, (1, 1, 2 * rank), 2) < rank
    flat_piece = jnp.where(low, m[:, 0], m[:, 1])
    half = blocks // 2
    flat_piece = flat_piece.reshape(GROUP, 2, half, ROWS, 128)
    for b in range(half):
        p_send[:, :, b * 128:(b + 1) * 128] = (
            flat_piece[:, :, b].reshape(GROUP, 2 * ROWS, 128).astype(jnp.bfloat16)
        )

    def send_pieces(i, _):
        to = lax.rem(slot + i, GROUP)
        pltpu.make_async_remote_copy(
            p_send.at[to], p_recv.at[slot], p_ssem, p_rsem,
            device_id={"tok": base + to}, device_id_type=pl.DeviceIdType.MESH,
        ).start()
        return 0

    lax.fori_loop(1, GROUP, send_pieces, 0)
    p_recv[slot] = p_send[slot]

    others = pl.ds(0, n - 1)
    pltpu.make_async_copy(q_recv.at[others], q_recv.at[others], q_rsem).wait()
    pltpu.make_async_copy(o_recv.at[others], o_recv.at[others], o_rsem).wait()
    q_recv[me] = q_send[slot]
    o_recv[me] = o_send[0]
    for k in range(n):
        block = q_recv[k].astype(jnp.float32)
        for b in range(blocks):
            h, i = divmod(b, half)
            q_mat_f32[h * nq + k * nq_dev:h * nq + (k + 1) * nq_dev, i * 128:(i + 1) * 128] = (
                block[b * nq_dev:(b + 1) * nq_dev]
            )
        o_mat[k:k + 1, :] = o_recv[k].astype(jnp.float32)
    q_mat[...] = q_mat_f32[...].astype(jnp.bfloat16)
    wants = (o_mat[:, :GROUP * ROWS] == ids).astype(jnp.bfloat16)

    peers = pl.ds(0, GROUP - 1)
    pltpu.make_async_copy(p_recv.at[peers], p_recv.at[peers], p_rsem).wait()
    x = p_recv[...].reshape(GROUP * 2 * ROWS, half * 128)
    y = lax.dot_general(x, q_mat[...], NT, preferred_element_type=jnp.float32)
    y = y.reshape(GROUP, 2, ROWS, 2 * nq)
    part = (y[:, 0, :, :nq] + y[:, 1, :, nq:]).reshape(GROUP * ROWS, nq)
    rows = jnp.dot(
        jnp.concatenate([wants] * 3, axis=1),
        jnp.concatenate(split_bf16(part, 3), axis=0),
        preferred_element_type=jnp.float32,
    )
    for k in range(n):
        s_send[k] = rows[k:k + 1, :]

    def send_scores(i, _):
        to = lax.rem(me + i, n)
        pltpu.make_async_remote_copy(
            s_send.at[to], s_recv.at[me], s_ssem, s_rsem,
            device_id={"tok": to}, device_id_type=pl.DeviceIdType.MESH,
        ).start()
        return 0

    lax.fori_loop(1, n, send_scores, 0)
    s_recv[me] = s_send[me]

    seq = lax.broadcasted_iota(jnp.int32, (1, seqs), 1)
    found = jnp.sum(jnp.where(seq == own, len_row, 0.0), axis=1, keepdims=True)
    scale = 1.0 / (rank * jnp.sqrt(jnp.maximum(found, 1.0)))

    pltpu.make_async_copy(s_recv.at[others], s_recv.at[others], s_rsem).wait()
    out[...] = jnp.sum(s_recv[...], axis=0) * scale

    pltpu.make_async_copy(q_recv.at[others], q_recv.at[others], q_ssem).wait()
    pltpu.make_async_copy(o_recv.at[others], o_recv.at[others], o_ssem).wait()
    pltpu.make_async_copy(p_recv.at[peers], p_recv.at[peers], p_ssem).wait()
    pltpu.make_async_copy(s_recv.at[others], s_recv.at[others], s_ssem).wait()


def on_device(n, acts, grads_out, proj_in, proj_out, lengths, owned, queries):
    tok, width = acts.shape
    rank = proj_in.shape[1]
    nq_dev = queries.shape[0]
    nq = nq_dev * n
    span = rank * rank // GROUP
    q_rows = nq_dev * span // 128
    bf16, f32, i32 = jnp.bfloat16, jnp.float32, jnp.int32
    hbm = pl.BlockSpec(memory_space=pl.ANY)
    vmem = pl.BlockSpec(memory_space=pltpu.VMEM)
    smem = pl.BlockSpec(memory_space=pltpu.SMEM)
    return pl.pallas_call(
        functools.partial(kernel, n),
        out_shape=jax.ShapeDtypeStruct((1, nq), f32),
        in_specs=[hbm, hbm, hbm, hbm, vmem, smem, vmem],
        out_specs=vmem,
        scratch_shapes=[
            pltpu.VMEM((tok, width), bf16),
            pltpu.VMEM((tok, width), bf16),
            pltpu.VMEM((rank, width), bf16),
            pltpu.VMEM((rank, width), bf16),
            pltpu.VMEM((GROUP, q_rows, 128), f32),
            pltpu.VMEM((GROUP, q_rows, 128), bf16),
            pltpu.VMEM((n, q_rows, 128), bf16),
            pltpu.VMEM((2 * nq, span // 2), f32),
            pltpu.VMEM((2 * nq, span // 2), bf16),
            pltpu.VMEM((1, 1, 128), i32),
            pltpu.VMEM((n, 1, 128), i32),
            pltpu.VMEM((n, 128), f32),
            pltpu.VMEM((GROUP, 2 * ROWS, span // 2), bf16),
            pltpu.VMEM((GROUP, 2 * ROWS, span // 2), bf16),
            pltpu.VMEM((n, 1, nq), f32),
            pltpu.VMEM((n, 1, nq), f32),
            pltpu.SemaphoreType.DMA((CHUNKS, 4)),
        ] + [pltpu.SemaphoreType.DMA] * 8,
        compiler_params=pltpu.CompilerParams(
            collective_id=0, has_side_effects=True, vmem_limit_bytes=48 * 1024 * 1024
        ),
    )(acts, grads_out, proj_in.T, proj_out.T, lengths.reshape(1, -1), owned, queries)


def solution(mesh):
    return jax.shard_map(
        functools.partial(on_device, mesh.shape["tok"]),
        mesh=mesh,
        in_specs=(
            P(("groups", "tok"), None),
            P(("groups", "tok"), None),
            P(),
            P(),
            P("groups"),
            P(("groups", "tok")),
            P(("groups", "tok"), None),
        ),
        out_specs=P(("groups", "tok"), None),
        check_vma=False,
    )
```

```python
import functools

import jax
import jax.numpy as jnp
from jax import lax
from jax.experimental import pallas as pl
from jax.experimental.pallas import tpu as pltpu
from jax.sharding import PartitionSpec as P

GROUP = 8
ROWS = 8
CHUNKS = 1
MEET = 0
VMEM_LIMIT = 62 * 1024 * 1024
NT = (((1,), (1,)), ((), ()))


def split_bf16(x, parts):
    out = []
    for _ in range(parts):
        head = x.astype(jnp.bfloat16)
        out.append(head)
        x = x - head.astype(jnp.float32)
    return out


def kernel(
    n, acts, grads, pin, pout, lengths_hbm, owned, queries_hbm, out,
    lengths, queries, a_buf, g_buf, pi_buf, po_buf, q_f32, q_send, q_recv, q_mat_f32, q_mat,
    o_send, o_recv, o_mat, p_send, p_recv, s_send, s_recv,
    small_sem, load_sem, q_ssem, q_rsem, o_ssem, o_rsem, p_ssem, p_rsem, s_ssem, s_rsem,
):
    me = lax.axis_index("tok")
    tok, width = a_buf.shape
    rank = pi_buf.shape[0]
    step = width // CHUNKS
    nq_dev = queries.shape[0]
    nq = nq_dev * n
    seqs = lengths.shape[1]
    flat = rank * rank
    span = flat // GROUP
    blocks = span // 128
    base = lax.div(me, GROUP) * GROUP
    slot = lax.rem(me, GROUP)

    small = [
        pltpu.make_async_copy(queries_hbm, queries, small_sem.at[0]),
        pltpu.make_async_copy(lengths_hbm, lengths, small_sem.at[1]),
    ]
    for c in small:
        c.start()
    loads = []
    for i in range(CHUNKS):
        cols = pl.ds(i * step, step)
        group = [
            pltpu.make_async_copy(src.at[:, cols], dst.at[:, cols], load_sem.at[i, j])
            for j, (src, dst) in enumerate(
                ((pout, po_buf), (grads, g_buf), (pin, pi_buf), (acts, a_buf))
            )
        ]
        for c in group:
            c.start()
        loads.append(group)

    barrier = pltpu.get_barrier_semaphore()

    def greet(i, _):
        pl.semaphore_signal(
            barrier, inc=1, device_id={"tok": lax.rem(me + i, n)},
            device_id_type=pl.DeviceIdType.MESH,
        )
        return 0

    lax.fori_loop(1, n, greet, 0, unroll=True)

    small[0].wait()
    small[1].wait()
    for a in range(GROUP):
        for b in range(blocks):
            q_f32[a, b * nq_dev:(b + 1) * nq_dev, :] = queries[
                :, (a * blocks + b) * 128:(a * blocks + b + 1) * 128
            ].astype(jnp.float32)
    q_send[...] = q_f32[...].astype(jnp.bfloat16)
    own = owned[0]
    o_send[...] = jnp.full(o_send.shape, own, jnp.int32)

    def send_queries(i, _):
        to = lax.rem(me + i, n)
        pltpu.make_async_remote_copy(
            q_send.at[lax.rem(to, GROUP)], q_recv.at[me], q_ssem, q_rsem,
            device_id={"tok": to}, device_id_type=pl.DeviceIdType.MESH,
        ).start()
        pltpu.make_async_remote_copy(
            o_send.at[0], o_recv.at[me], o_ssem, o_rsem,
            device_id={"tok": to}, device_id_type=pl.DeviceIdType.MESH,
        ).start()
        return 0

    len_row = lengths[...].astype(jnp.float32)
    row_i = lax.broadcasted_iota(jnp.int32, (seqs, seqs), 0)
    col_i = lax.broadcasted_iota(jnp.int32, (seqs, seqs), 1)
    ends = jnp.sum(jnp.where(col_i <= row_i, len_row, 0.0), axis=1, keepdims=True)
    pos = (me * tok + lax.broadcasted_iota(jnp.int32, (1, tok), 1)).astype(jnp.float32)
    seq_of = jnp.sum((ends <= pos).astype(jnp.float32), axis=0, keepdims=True)
    start = (me * tok).astype(jnp.float32)
    first = jnp.sum((ends <= start).astype(jnp.float32), axis=0, keepdims=True)
    piece = lax.broadcasted_iota(jnp.int32, (ROWS, tok), 0).astype(jnp.float32)
    member = ((seq_of - first) == piece).astype(jnp.float32)
    lane = lax.broadcasted_iota(jnp.int32, (1, GROUP * ROWS), 1)
    shard_start = ((base + lane // ROWS) * tok).astype(jnp.float32)
    ids = jnp.sum((ends <= shard_start).astype(jnp.float32), axis=0, keepdims=True)
    ids = ids + (lane % ROWS).astype(jnp.float32)

    g_t = jnp.zeros((rank, tok), jnp.float32)
    a_t = jnp.zeros((rank, tok), jnp.float32)
    for i in range(CHUNKS):
        if i == MEET:
            pl.semaphore_wait(barrier, n - 1)
            lax.fori_loop(1, n, send_queries, 0, unroll=True)
        cols = pl.ds(i * step, step)
        loads[i][0].wait()
        loads[i][1].wait()
        g_t += lax.dot_general(
            po_buf[:, cols], g_buf[:, cols], NT, preferred_element_type=jnp.float32
        )
        loads[i][2].wait()
        loads[i][3].wait()
        a_t += lax.dot_general(
            pi_buf[:, cols], a_buf[:, cols], NT, preferred_element_type=jnp.float32
        )

    g_hi, g_lo = [
        (part.astype(jnp.float32)[:, None, :] * member[None]).reshape(rank * ROWS, tok)
        .astype(jnp.bfloat16)
        for part in split_bf16(g_t, 2)
    ]
    a_hi, a_lo = split_bf16(a_t, 2)
    both = jnp.concatenate([a_hi, a_hi, a_lo, a_lo], axis=0)
    m = lax.dot_general(g_hi, both, NT, preferred_element_type=jnp.float32)
    m = m[:, :2 * rank] + m[:, 2 * rank:] + lax.dot_general(
        g_lo, both[:2 * rank], NT, preferred_element_type=jnp.float32
    )
    m = m.reshape(rank // 2, 2, ROWS, 2 * rank)
    low = lax.broadcasted_iota(jnp.int32, (1, 1, 2 * rank), 2) < rank
    flat_piece = jnp.where(low, m[:, 0], m[:, 1])
    half = blocks // 2
    flat_piece = flat_piece.reshape(GROUP, 2, half, ROWS, 128)
    for b in range(half):
        p_send[:, :, b * 128:(b + 1) * 128] = (
            flat_piece[:, :, b].reshape(GROUP, 2 * ROWS, 128).astype(jnp.bfloat16)
        )

    def send_pieces(i, _):
        to = lax.rem(slot + i, GROUP)
        pltpu.make_async_remote_copy(
            p_send.at[to], p_recv.at[slot], p_ssem, p_rsem,
            device_id={"tok": base + to}, device_id_type=pl.DeviceIdType.MESH,
        ).start()
        return 0

    lax.fori_loop(1, GROUP, send_pieces, 0, unroll=True)
    p_recv[slot] = p_send[slot]

    others = pl.ds(0, n - 1)
    pltpu.make_async_copy(q_recv.at[others], q_recv.at[others], q_rsem).wait()
    pltpu.make_async_copy(o_recv.at[others], o_recv.at[others], o_rsem).wait()
    q_recv[me] = q_send[slot]
    o_recv[me] = o_send[0]
    for k in range(n):
        block = q_recv[k].astype(jnp.float32)
        for b in range(blocks):
            h, i = divmod(b, half)
            q_mat_f32[h * nq + k * nq_dev:h * nq + (k + 1) * nq_dev, i * 128:(i + 1) * 128] = (
                block[b * nq_dev:(b + 1) * nq_dev]
            )
        o_mat[k:k + 1, :] = o_recv[k].astype(jnp.float32)
    q_mat[...] = q_mat_f32[...].astype(jnp.bfloat16)
    wants = (o_mat[:, :GROUP * ROWS] == ids).astype(jnp.bfloat16)

    peers = pl.ds(0, GROUP - 1)
    pltpu.make_async_copy(p_recv.at[peers], p_recv.at[peers], p_rsem).wait()
    x = p_recv[...].reshape(GROUP * 2 * ROWS, half * 128)
    y = lax.dot_general(x, q_mat[...], NT, preferred_element_type=jnp.float32)
    y = y.reshape(GROUP, 2, ROWS, 2 * nq)
    part = (y[:, 0, :, :nq] + y[:, 1, :, nq:]).reshape(GROUP * ROWS, nq)
    rows = jnp.dot(
        jnp.concatenate([wants] * 3, axis=1),
        jnp.concatenate(split_bf16(part, 3), axis=0),
        preferred_element_type=jnp.float32,
    )
    for k in range(n):
        s_send[k] = rows[k:k + 1, :]

    def send_scores(i, _):
        to = lax.rem(me + i, n)
        pltpu.make_async_remote_copy(
            s_send.at[to], s_recv.at[me], s_ssem, s_rsem,
            device_id={"tok": to}, device_id_type=pl.DeviceIdType.MESH,
        ).start()
        return 0

    lax.fori_loop(1, n, send_scores, 0, unroll=True)
    s_recv[me] = s_send[me]

    seq = lax.broadcasted_iota(jnp.int32, (1, seqs), 1)
    found = jnp.sum(jnp.where(seq == own, len_row, 0.0), axis=1, keepdims=True)
    scale = 1.0 / (rank * jnp.sqrt(jnp.maximum(found, 1.0)))

    pltpu.make_async_copy(s_recv.at[others], s_recv.at[others], s_rsem).wait()
    out[...] = jnp.sum(s_recv[...], axis=0) * scale

    pltpu.make_async_copy(q_recv.at[others], q_recv.at[others], q_ssem).wait()
    pltpu.make_async_copy(o_recv.at[others], o_recv.at[others], o_ssem).wait()
    pltpu.make_async_copy(p_recv.at[peers], p_recv.at[peers], p_ssem).wait()
    pltpu.make_async_copy(s_recv.at[others], s_recv.at[others], s_ssem).wait()


def on_device(n, acts, grads_out, proj_in, proj_out, lengths, owned, queries):
    lengths = lengths.reshape(1, -1)
    tok, width = acts.shape
    rank = proj_in.shape[1]
    nq_dev = queries.shape[0]
    nq = nq_dev * n
    span = rank * rank // GROUP
    q_rows = nq_dev * span // 128
    bf16, f32, i32 = jnp.bfloat16, jnp.float32, jnp.int32
    hbm = pl.BlockSpec(memory_space=pltpu.HBM)
    vmem = pl.BlockSpec(memory_space=pltpu.VMEM)
    smem = pl.BlockSpec(memory_space=pltpu.SMEM)
    return pl.pallas_call(
        functools.partial(kernel, n),
        out_shape=jax.ShapeDtypeStruct((1, nq), f32),
        in_specs=[hbm, hbm, hbm, hbm, hbm, smem, hbm],
        out_specs=vmem,
        scratch_shapes=[
            pltpu.VMEM(lengths.shape, i32),
            pltpu.VMEM(queries.shape, bf16),
            pltpu.VMEM((tok, width), bf16),
            pltpu.VMEM((tok, width), bf16),
            pltpu.VMEM((rank, width), bf16),
            pltpu.VMEM((rank, width), bf16),
            pltpu.VMEM((GROUP, q_rows, 128), f32),
            pltpu.VMEM((GROUP, q_rows, 128), bf16),
            pltpu.VMEM((n, q_rows, 128), bf16),
            pltpu.VMEM((2 * nq, span // 2), f32),
            pltpu.VMEM((2 * nq, span // 2), bf16),
            pltpu.VMEM((1, 1, 128), i32),
            pltpu.VMEM((n, 1, 128), i32),
            pltpu.VMEM((n, 128), f32),
            pltpu.VMEM((GROUP, 2 * ROWS, span // 2), bf16),
            pltpu.VMEM((GROUP, 2 * ROWS, span // 2), bf16),
            pltpu.VMEM((n, 1, nq), f32),
            pltpu.VMEM((n, 1, nq), f32),
            pltpu.SemaphoreType.DMA((2,)),
            pltpu.SemaphoreType.DMA((CHUNKS, 4)),
        ] + [pltpu.SemaphoreType.DMA] * 8,
        compiler_params=pltpu.CompilerParams(
            collective_id=0, has_side_effects=True, vmem_limit_bytes=VMEM_LIMIT
        ),
    )(acts, grads_out, proj_in.T, proj_out.T, lengths, owned, queries)


def solution(mesh):
    return jax.shard_map(
        functools.partial(on_device, mesh.shape["tok"]),
        mesh=mesh,
        in_specs=(
            P(("groups", "tok"), None),
            P(("groups", "tok"), None),
            P(),
            P(),
            P("groups"),
            P(("groups", "tok")),
            P(("groups", "tok"), None),
        ),
        out_specs=P(("groups", "tok"), None),
        check_vma=False,
    )
```

```python
import functools

import jax
import jax.numpy as jnp
from jax import lax
from jax.experimental import pallas as pl
from jax.experimental.pallas import tpu as pltpu
from jax.sharding import PartitionSpec as P

GROUP = 8
ROWS = 8
CHUNKS = 1
MEET = 0
VMEM_LIMIT = 62 * 1024 * 1024
NT = (((1,), (1,)), ((), ()))


def split_bf16(x, parts):
    out = []
    for _ in range(parts):
        head = x.astype(jnp.bfloat16)
        out.append(head)
        x = x - head.astype(jnp.float32)
    return out


def kernel(
    n, acts, grads, pin, pout, lengths_hbm, owned, queries_hbm, out,
    lengths, queries, a_buf, g_buf, pi_buf, po_buf, q_f32, q_send, q_recv, q_mat_f32, q_mat,
    o_send, o_recv, o_mat, p_send, p_recv, s_send, s_recv,
    small_sem, load_sem, q_ssem, q_rsem, o_ssem, o_rsem, p_ssem, p_rsem, s_ssem, s_rsem,
):
    me = lax.axis_index("tok")
    tok, width = a_buf.shape
    rank = pi_buf.shape[0]
    step = width // CHUNKS
    nq_dev = queries.shape[0]
    nq = nq_dev * n
    seqs = lengths.shape[1]
    flat = rank * rank
    span = flat // GROUP
    blocks = span // 128
    base = lax.div(me, GROUP) * GROUP
    slot = lax.rem(me, GROUP)

    barrier = pltpu.get_barrier_semaphore()

    def greet(i, _):
        pl.semaphore_signal(
            barrier, inc=1, device_id={"tok": lax.rem(me + i, n)},
            device_id_type=pl.DeviceIdType.MESH,
        )
        return 0

    lax.fori_loop(1, n, greet, 0, unroll=True)

    small = [
        pltpu.make_async_copy(queries_hbm, queries, small_sem.at[0]),
        pltpu.make_async_copy(lengths_hbm, lengths, small_sem.at[1]),
    ]
    for c in small:
        c.start()
    loads = []
    for i in range(CHUNKS):
        cols = pl.ds(i * step, step)
        group = [
            pltpu.make_async_copy(src.at[:, cols], dst.at[:, cols], load_sem.at[i, j])
            for j, (src, dst) in enumerate(
                ((pout, po_buf), (grads, g_buf), (pin, pi_buf), (acts, a_buf))
            )
        ]
        for c in group:
            c.start()
        loads.append(group)

    small[0].wait()
    small[1].wait()
    for a in range(GROUP):
        for b in range(blocks):
            q_f32[a, b * nq_dev:(b + 1) * nq_dev, :] = queries[
                :, (a * blocks + b) * 128:(a * blocks + b + 1) * 128
            ].astype(jnp.float32)
    q_send[...] = q_f32[...].astype(jnp.bfloat16)
    own = owned[0]
    o_send[...] = jnp.full(o_send.shape, own, jnp.int32)

    def send_queries(i, _):
        to = lax.rem(me + i, n)
        pltpu.make_async_remote_copy(
            q_send.at[lax.rem(to, GROUP)], q_recv.at[me], q_ssem, q_rsem,
            device_id={"tok": to}, device_id_type=pl.DeviceIdType.MESH,
        ).start()
        pltpu.make_async_remote_copy(
            o_send.at[0], o_recv.at[me], o_ssem, o_rsem,
            device_id={"tok": to}, device_id_type=pl.DeviceIdType.MESH,
        ).start()
        return 0

    len_row = lengths[...].astype(jnp.float32)
    row_i = lax.broadcasted_iota(jnp.int32, (seqs, seqs), 0)
    col_i = lax.broadcasted_iota(jnp.int32, (seqs, seqs), 1)
    ends = jnp.sum(jnp.where(col_i <= row_i, len_row, 0.0), axis=1, keepdims=True)
    pos = (me * tok + lax.broadcasted_iota(jnp.int32, (1, tok), 1)).astype(jnp.float32)
    seq_of = jnp.sum((ends <= pos).astype(jnp.float32), axis=0, keepdims=True)
    start = (me * tok).astype(jnp.float32)
    first = jnp.sum((ends <= start).astype(jnp.float32), axis=0, keepdims=True)
    piece = lax.broadcasted_iota(jnp.int32, (ROWS, tok), 0).astype(jnp.float32)
    member = ((seq_of - first) == piece).astype(jnp.float32)
    lane = lax.broadcasted_iota(jnp.int32, (1, GROUP * ROWS), 1)
    shard_start = ((base + lane // ROWS) * tok).astype(jnp.float32)
    ids = jnp.sum((ends <= shard_start).astype(jnp.float32), axis=0, keepdims=True)
    ids = ids + (lane % ROWS).astype(jnp.float32)

    g_t = jnp.zeros((rank, tok), jnp.float32)
    a_t = jnp.zeros((rank, tok), jnp.float32)
    for i in range(CHUNKS):
        if i == MEET:
            pl.semaphore_wait(barrier, n - 1)
            lax.fori_loop(1, n, send_queries, 0, unroll=True)
        cols = pl.ds(i * step, step)
        loads[i][0].wait()
        loads[i][1].wait()
        g_t += lax.dot_general(
            po_buf[:, cols], g_buf[:, cols], NT, preferred_element_type=jnp.float32
        )
        loads[i][2].wait()
        loads[i][3].wait()
        a_t += lax.dot_general(
            pi_buf[:, cols], a_buf[:, cols], NT, preferred_element_type=jnp.float32
        )

    g_hi, g_lo = [
        (part.astype(jnp.float32)[:, None, :] * member[None]).reshape(rank * ROWS, tok)
        .astype(jnp.bfloat16)
        for part in split_bf16(g_t, 2)
    ]
    a_hi, a_lo = split_bf16(a_t, 2)
    both = jnp.concatenate([a_hi, a_hi, a_lo, a_lo], axis=0)
    m = lax.dot_general(g_hi, both, NT, preferred_element_type=jnp.float32)
    m = m[:, :2 * rank] + m[:, 2 * rank:] + lax.dot_general(
        g_lo, both[:2 * rank], NT, preferred_element_type=jnp.float32
    )
    m = m.reshape(rank // 2, 2, ROWS, 2 * rank)
    low = lax.broadcasted_iota(jnp.int32, (1, 1, 2 * rank), 2) < rank
    flat_piece = jnp.where(low, m[:, 0], m[:, 1])
    half = blocks // 2
    flat_piece = flat_piece.reshape(GROUP, 2, half, ROWS, 128)
    for b in range(half):
        p_send[:, :, b * 128:(b + 1) * 128] = (
            flat_piece[:, :, b].reshape(GROUP, 2 * ROWS, 128).astype(jnp.bfloat16)
        )

    def send_pieces(i, _):
        to = lax.rem(slot + i, GROUP)
        pltpu.make_async_remote_copy(
            p_send.at[to], p_recv.at[slot], p_ssem, p_rsem,
            device_id={"tok": base + to}, device_id_type=pl.DeviceIdType.MESH,
        ).start()
        return 0

    lax.fori_loop(1, GROUP, send_pieces, 0, unroll=True)
    p_recv[slot] = p_send[slot]

    others = pl.ds(0, n - 1)
    pltpu.make_async_copy(q_recv.at[others], q_recv.at[others], q_rsem).wait()
    pltpu.make_async_copy(o_recv.at[others], o_recv.at[others], o_rsem).wait()
    q_recv[me] = q_send[slot]
    o_recv[me] = o_send[0]
    for k in range(n):
        block = q_recv[k].astype(jnp.float32)
        for b in range(blocks):
            h, i = divmod(b, half)
            q_mat_f32[h * nq + k * nq_dev:h * nq + (k + 1) * nq_dev, i * 128:(i + 1) * 128] = (
                block[b * nq_dev:(b + 1) * nq_dev]
            )
        o_mat[k:k + 1, :] = o_recv[k].astype(jnp.float32)
    q_mat[...] = q_mat_f32[...].astype(jnp.bfloat16)
    wants = (o_mat[:, :GROUP * ROWS] == ids).astype(jnp.bfloat16)

    peers = pl.ds(0, GROUP - 1)
    pltpu.make_async_copy(p_recv.at[peers], p_recv.at[peers], p_rsem).wait()
    x = p_recv[...].reshape(GROUP * 2 * ROWS, half * 128)
    y = lax.dot_general(x, q_mat[...], NT, preferred_element_type=jnp.float32)
    y = y.reshape(GROUP, 2, ROWS, 2 * nq)
    part = (y[:, 0, :, :nq] + y[:, 1, :, nq:]).reshape(GROUP * ROWS, nq)
    rows = jnp.dot(
        jnp.concatenate([wants] * 3, axis=1),
        jnp.concatenate(split_bf16(part, 3), axis=0),
        preferred_element_type=jnp.float32,
    )
    for k in range(n):
        s_send[k] = rows[k:k + 1, :]

    def send_scores(i, _):
        to = lax.rem(me + i, n)
        pltpu.make_async_remote_copy(
            s_send.at[to], s_recv.at[me], s_ssem, s_rsem,
            device_id={"tok": to}, device_id_type=pl.DeviceIdType.MESH,
        ).start()
        return 0

    lax.fori_loop(1, n, send_scores, 0, unroll=True)
    s_recv[me] = s_send[me]

    seq = lax.broadcasted_iota(jnp.int32, (1, seqs), 1)
    found = jnp.sum(jnp.where(seq == own, len_row, 0.0), axis=1, keepdims=True)
    scale = 1.0 / (rank * jnp.sqrt(jnp.maximum(found, 1.0)))

    pltpu.make_async_copy(s_recv.at[others], s_recv.at[others], s_rsem).wait()
    out[...] = jnp.sum(s_recv[...], axis=0) * scale

    pltpu.make_async_copy(q_recv.at[others], q_recv.at[others], q_ssem).wait()
    pltpu.make_async_copy(o_recv.at[others], o_recv.at[others], o_ssem).wait()
    pltpu.make_async_copy(p_recv.at[peers], p_recv.at[peers], p_ssem).wait()
    pltpu.make_async_copy(s_recv.at[others], s_recv.at[others], s_ssem).wait()


def on_device(n, acts, grads_out, proj_in, proj_out, lengths, owned, queries):
    lengths = lengths.reshape(1, -1)
    tok, width = acts.shape
    rank = proj_in.shape[1]
    nq_dev = queries.shape[0]
    nq = nq_dev * n
    span = rank * rank // GROUP
    q_rows = nq_dev * span // 128
    bf16, f32, i32 = jnp.bfloat16, jnp.float32, jnp.int32
    hbm = pl.BlockSpec(memory_space=pltpu.HBM)
    vmem = pl.BlockSpec(memory_space=pltpu.VMEM)
    smem = pl.BlockSpec(memory_space=pltpu.SMEM)
    return pl.pallas_call(
        functools.partial(kernel, n),
        out_shape=jax.ShapeDtypeStruct((1, nq), f32),
        in_specs=[hbm, hbm, hbm, hbm, hbm, smem, hbm],
        out_specs=vmem,
        scratch_shapes=[
            pltpu.VMEM(lengths.shape, i32),
            pltpu.VMEM(queries.shape, bf16),
            pltpu.VMEM((tok, width), bf16),
            pltpu.VMEM((tok, width), bf16),
            pltpu.VMEM((rank, width), bf16),
            pltpu.VMEM((rank, width), bf16),
            pltpu.VMEM((GROUP, q_rows, 128), f32),
            pltpu.VMEM((GROUP, q_rows, 128), bf16),
            pltpu.VMEM((n, q_rows, 128), bf16),
            pltpu.VMEM((2 * nq, span // 2), f32),
            pltpu.VMEM((2 * nq, span // 2), bf16),
            pltpu.VMEM((1, 1, 128), i32),
            pltpu.VMEM((n, 1, 128), i32),
            pltpu.VMEM((n, 128), f32),
            pltpu.VMEM((GROUP, 2 * ROWS, span // 2), bf16),
            pltpu.VMEM((GROUP, 2 * ROWS, span // 2), bf16),
            pltpu.VMEM((n, 1, nq), f32),
            pltpu.VMEM((n, 1, nq), f32),
            pltpu.SemaphoreType.DMA((2,)),
            pltpu.SemaphoreType.DMA((CHUNKS, 4)),
        ] + [pltpu.SemaphoreType.DMA] * 8,
        compiler_params=pltpu.CompilerParams(
            collective_id=0, has_side_effects=True, vmem_limit_bytes=VMEM_LIMIT
        ),
    )(acts, grads_out, proj_in.T, proj_out.T, lengths, owned, queries)


def solution(mesh):
    return jax.shard_map(
        functools.partial(on_device, mesh.shape["tok"]),
        mesh=mesh,
        in_specs=(
            P(("groups", "tok"), None),
            P(("groups", "tok"), None),
            P(),
            P(),
            P("groups"),
            P(("groups", "tok")),
            P(("groups", "tok"), None),
        ),
        out_specs=P(("groups", "tok"), None),
        check_vma=False,
    )
```
